512 devices in a mesh: view: 32 (over y_hi, z), tok: 16 (over x, y_lo, core).
Axes of the slice: x: 4, y: 4 (y_hi: 2, y_lo: 2; y = y_hi * 2 + y_lo), z: 16, core: 2. Of those that a mesh axis runs over, the one named last changes fastest.
Arguments:
- queries: bfloat16 [32, 2, 2048, 1024], P('view', None, 'tok'), may hold values from -6 to 6
- keys: bfloat16 [32, 2, 2048, 1024], P('view', None, 'tok'), may hold values from -6 to 6
- values: bfloat16 [32, 2, 2048, 1024], P('view', None, 'tok'), may hold values from -6 to 6
- tile_mask: int32 [32, 2, 16, 16], P('view'), may hold values from 0 to 1, as said below
- offsets: int32 [32, 2], P('view'), may hold values from -2 to 2, as said below
- branch_slots: int32 [32, 2], replicated, may hold values from 0 to 1, each once within a row
Outputs:
- attended: bfloat16 [32, 2, 2048, 1024], P('view', None, 'tok')
The draws below stay inside these ranges and needn't reach their ends.
Inputs may be any that keep to these rules, and one draw needn't show every extreme that they name: Each row tile_mask[v, j, t, :] holds 1 to 6 ones at consecutive tiles modulo 16; for every v and j some row holds exactly 6. `offsets`: each row holds two different values of -2, -1, 1, 2. `branch_slots`: each row is 0, 1 or 1, 0.
All inputs are finite; a program needn't handle non-finite values.
Results may differ from the reference program's by a relative error of at most 0.0049.
Values may be sent and summed in bfloat16 or wider, within the bound.
A program may use at most 64 MiB of HBM per device.

```python
import jax
import jax.numpy as jnp
from jax import lax

HD = 64
HEADS = 16
TILE = 128
NB = 2
VIEWS = 32
VIEW_TOK = 2048
W = 1024
KT = 16
MOST = 6


def draw_queries(key, part):
    key = jax.random.fold_in(key, 11)
    shape = (VIEWS, 2, VIEW_TOK, W)
    base = jnp.clip(jax.random.normal(key, shape), -6.0, 6.0)
    return base.astype(jnp.bfloat16)


def draw_keys(key, part):
    key = jax.random.fold_in(key, 23)
    shape = (VIEWS, 2, VIEW_TOK, W)
    base = jnp.clip(jax.random.normal(key, shape), -6.0, 6.0)
    return base.astype(jnp.bfloat16)


def draw_tile_mask(key, part):
    key = jax.random.fold_in(key, 37)
    first, second, third = jax.random.split(key, 3)
    counts = jax.random.randint(first, (VIEWS, NB, KT), 1, MOST + 1)
    full_at = jax.random.randint(second, (VIEWS, NB), 0, KT)
    counts = jnp.where(jnp.arange(KT)[None, None, :] == full_at[..., None], MOST, counts)
    start = jax.random.randint(third, (VIEWS, NB, KT), 0, KT)
    position = (jnp.arange(KT)[None, None, None, :] - start[..., None]) % KT
    return (position < counts[..., None]).astype(jnp.int32)


def draw_offsets(key, part):
    key = jax.random.fold_in(key, 51)
    view_keys = jax.random.split(key, VIEWS)
    orders = jax.vmap(lambda single: jax.random.permutation(single, 4))(view_keys)
    table = jnp.array([-2, -1, 1, 2], jnp.int32)
    return table[orders[:, :NB]]


def block_levels(own_key, dims, cuts, least, top_value):
    level = 1.0
    for axis_at, parts in cuts:
        heights = jax.random.uniform(jax.random.fold_in(jax.random.fold_in(own_key, 6), axis_at), (parts,), jnp.float32, least / len(cuts), top_value / len(cuts))
        level = level * jnp.repeat(jnp.exp(heights), dims[axis_at] // parts).reshape((-1,) + (1,) * (len(dims) - 1 - axis_at))
    return level


def scatter_about(key, extent, spread, bound, pieces=(), kind=jnp.bfloat16):
    values = spread * jax.random.normal(key, extent, jnp.float32)
    if pieces:
        values = values * block_levels(key, extent, pieces, -0.22, 0.18)
    return jnp.clip(values, -bound, bound).astype(kind)


def setup_inputs(seed: int = 0) -> dict:
    seeds = jax.random.split(jax.random.key(seed), 7)
    queries = draw_queries(jax.random.fold_in(seeds[6], 71), 0)
    keys = draw_keys(jax.random.fold_in(seeds[6], 71), 0)
    values = scatter_about(seeds[2], (VIEWS, 2, VIEW_TOK, W), 1.0, 6.0, ((0, 32), (2, 16)))
    tile_mask = draw_tile_mask(jax.random.fold_in(seeds[6], 71), 0)
    offsets = draw_offsets(jax.random.fold_in(seeds[6], 71), 0)
    branch_slots = jax.vmap(lambda own: jax.random.permutation(own, 2))(jax.random.split(seeds[5], VIEWS)).reshape((VIEWS, 2)).astype(jnp.int32)
    return dict(queries=queries, keys=keys, values=values, tile_mask=tile_mask, offsets=offsets, branch_slots=branch_slots)


NEG_SCORE = -1e30


def attend_tile(query_tile, key_block, value_block, keep_mask):
    scores = jnp.einsum("bqhd,bkhd->bhqk", query_tile, key_block) * (HD ** -0.5)
    scores = jnp.where(keep_mask[None, None, None, :], scores, NEG_SCORE)
    row_max = jnp.max(scores, axis=-1, keepdims=True)
    expo = jnp.exp(scores - row_max)
    row_total = jnp.sum(expo, axis=-1, keepdims=True)
    weights = lax.optimization_barrier((expo / row_total).astype(jnp.bfloat16)).astype(jnp.float32)
    result = jnp.einsum("bhqk,bkhd->bqhd", weights, value_block)
    return result.astype(jnp.bfloat16)


def reference(queries, keys, values, tile_mask, offsets, branch_slots):
    tile_count = jnp.sum(tile_mask, axis=-1)
    chosen = jnp.argsort(1 - tile_mask, axis=-1, stable=True)[..., :MOST].astype(jnp.int32)
    valid = jnp.arange(MOST, dtype=jnp.int32)[None, None, None, :] < tile_count[..., None]

    def view_result(view_index):
        shape5 = (2, KT, TILE, HEADS, HD)
        query_all = queries[view_index].astype(jnp.float32).reshape(shape5)
        own_keys = keys[view_index].astype(jnp.float32).reshape(shape5)
        own_values = values[view_index].astype(jnp.float32).reshape(shape5)
        other_keys = []
        other_values = []
        for member in range(NB):
            other_view = (view_index + offsets[view_index, member]) % VIEWS
            flipped = branch_slots[other_view, 0] != branch_slots[view_index, 0]
            key_other = keys[other_view]
            value_other = values[other_view]
            key_other = jnp.where(flipped, key_other[::-1], key_other)
            value_other = jnp.where(flipped, value_other[::-1], value_other)
            other_keys.append(key_other.astype(jnp.float32).reshape(shape5))
            other_values.append(value_other.astype(jnp.float32).reshape(shape5))

        def tile_result(tile_index):
            key_parts = [own_keys[:, tile_index]]
            value_parts = [own_values[:, tile_index]]
            keep_parts = [jnp.ones((TILE,), bool)]
            for member in range(NB):
                picked = chosen[view_index, member, tile_index]
                key_parts.append(other_keys[member][:, picked].reshape(2, MOST * TILE, HEADS, HD))
                value_parts.append(other_values[member][:, picked].reshape(2, MOST * TILE, HEADS, HD))
                keep_parts.append(jnp.repeat(valid[view_index, member, tile_index], TILE))
            return attend_tile(query_all[:, tile_index], jnp.concatenate(key_parts, 1),
                               jnp.concatenate(value_parts, 1), jnp.concatenate(keep_parts))

        tiles_out = lax.map(tile_result, jnp.arange(KT, dtype=jnp.int32))
        return jnp.moveaxis(tiles_out, 0, 1).reshape(2, VIEW_TOK, W)

    return lax.map(view_result, jnp.arange(VIEWS, dtype=jnp.int32))
```

```python
import jax
import jax.numpy as jnp
from jax import lax
from jax.experimental import pallas as pl
from jax.experimental.pallas import tpu as pltpu
from jax.sharding import PartitionSpec as P

MESH = pl.DeviceIdType.MESH
TILE = 128
LANES = 128
HD = 64
BAND = 6
NB = 2
KEY_COLS = 1 + NB * BAND
NEG_SCORE = -1e30
XS = 4
ROWS = 64
GX = (0, 1, 3, 2)


def attend_kernel(
    mask_ref, off_ref, slot_ref, q_ref, k_ref, v_ref, out_ref,
    raw_k, raw_v, raw_q, stage, qbuf, kbuf, vbuf, sbuf, wbuf, obuf, orecv, ost, start_s, count_s,
    in_sem, a_send, a_recv, z_send, z_recv, o_send, o_recv, out_sem,
):
    views = lax.axis_size("view")
    toks = lax.axis_size("tok")
    group = toks // XS
    view = lax.axis_index("view")
    me = lax.axis_index("tok")
    right = lax.rem(view + 1, views)
    left = lax.rem(view + views - 1, views)
    my_x = me // group
    my_r = lax.rem(me, group)
    bufs = (kbuf, vbuf, qbuf)
    raws = (raw_k, raw_v, raw_q)

    def remote(src, dst, send, recv, dev):
        return pltpu.make_async_remote_copy(
            src_ref=src, dst_ref=dst, send_sem=send, recv_sem=recv, device_id=dev, device_id_type=MESH
        )

    def in_copy(a):
        return pltpu.make_async_copy((k_ref, v_ref, q_ref)[a].at[0], raws[a], in_sem.at[a])

    for a in range(3):
        in_copy(a).start()

    barrier = pltpu.get_barrier_semaphore()
    for d in range(1, 16):
        pl.semaphore_signal(barrier, inc=1, device_id=(view, lax.rem(me + d, toks)), device_id_type=MESH)
    for to in (right, left):
        pl.semaphore_signal(barrier, inc=1, device_id=(to, me), device_id_type=MESH)

    first_slot = slot_ref[view, 0]

    def stage_array(a):
        in_copy(a).wait()
        for b in range(2):
            slot = first_slot if b == 0 else 1 - first_slot
            for p in range(8):
                stage[a, p * 2 + b] = raws[a][slot, :, p * LANES:(p + 1) * LANES]
        bufs[a][me] = stage[a, me]

    def a2a_copy(a, dest):
        return remote(stage.at[a, dest], bufs[a].at[me], a_send.at[a, dest], a_recv.at[a, me], (view, dest))

    def a2a_send(a):
        for gx in GX:
            for r in range(4):
                if (gx, r) != (0, 0):
                    dest = lax.rem(my_x + gx, XS) * group + lax.rem(my_r + r, group)
                    a2a_copy(a, dest).start()

    def a2a_wait(a, gx):
        for r in range(4):
            if (gx, r) != (0, 0):
                src = lax.rem(my_x + XS - gx, XS) * group + lax.rem(my_r + group - r, group)
                remote(stage.at[a, 0], bufs[a].at[src], a_send.at[a, 0], a_recv.at[a, src], (view, src)).wait_recv()

    def z_copy(a, hop, gi, gx):
        start = lax.rem(my_x + XS - gx, XS) * group
        src_set, dst_set, dev = ((0, 1, right), (0, 2, left), (1, 3, right), (2, 4, left))[hop]
        return remote(
            bufs[a].at[pl.ds(src_set * toks + start, 4)],
            bufs[a].at[pl.ds(dst_set * toks + start, 4)],
            z_send.at[a, hop, gi], z_recv.at[a, hop, gi], (dev, me),
        )

    stage_array(0)
    pl.semaphore_wait(barrier, 17)
    a2a_send(0)
    a2a_wait(0, GX[0])
    for hop in (0, 1):
        z_copy(0, hop, 0, GX[0]).start()
    stage_array(1)
    a2a_send(1)
    a2a_wait(0, GX[1])
    for hop in (0, 1):
        z_copy(0, hop, 1, GX[1]).start()
    stage_array(2)
    a2a_send(2)
    for gi in (2, 3):
        a2a_wait(0, GX[gi])
        for hop in (0, 1):
            z_copy(0, hop, gi, GX[gi]).start()
    for gi in range(4):
        for hop in (0, 1):
            z_copy(0, hop, gi, GX[gi]).wait_recv()
            z_copy(0, hop + 2, gi, GX[gi]).start()
    for gi in range(4):
        a2a_wait(1, GX[gi])
        for hop in (0, 1):
            z_copy(1, hop, gi, GX[gi]).start()

    for j in range(NB):
        def count_row(t, carry, j=j):
            first = jnp.int32(0)
            total = jnp.int32(0)
            before = mask_ref[0, j, t, 15]
            for k in range(16):
                here = mask_ref[0, j, t, k]
                total = total + here
                first = first + jnp.where((here == 1) & (before == 0), k, 0)
                before = here
            start_s[j, t] = first
            count_s[j, t] = total
            return carry
        lax.fori_loop(0, 16, count_row, 0)

    for gx in GX:
        a2a_wait(2, gx)
    for gi in range(4):
        for hop in (2, 3):
            z_copy(0, hop, gi, GX[gi]).wait_recv()

    sets = []
    for j in range(NB):
        off = off_ref[0, j]
        sets.append(jnp.where(off == -1, 1, jnp.where(off == 1, 2, jnp.where(off == -2, 3, 4))) * toks)
    low = lax.broadcasted_iota(jnp.int32, (TILE, LANES), 1) < HD

    def tile_at(j, t, i):
        return sets[j] + lax.rem(start_s[j, t] + i, 16)

    def dot_t(x, y):
        return lax.dot_general(x, y, (((1,), (1,)), ((), ())), preferred_element_type=jnp.float32)

    def weigh_tile(t):
        q = qbuf[t] * jnp.bfloat16(0.125)
        zero = jnp.zeros_like(q)
        both = jnp.concatenate([jnp.where(low, q, zero), jnp.where(low, zero, q)], axis=0)
        sbuf[:, :LANES] = dot_t(both, kbuf[t])
        for j in range(NB):
            for i in range(0, BAND, 2):
                keys = jnp.concatenate([kbuf[tile_at(j, t, i)], kbuf[tile_at(j, t, i + 1)]], axis=0)
                s = dot_t(both, keys)
                for h in range(2):
                    bias = jnp.where(i + h < count_s[j, t], jnp.float32(0), jnp.float32(NEG_SCORE))
                    c = 1 + j * BAND + i + h
                    sbuf[:, c * LANES:(c + 1) * LANES] = s[:, h * LANES:(h + 1) * LANES] + bias
        for rb in range(0, 2 * TILE, ROWS):
            rows = pl.ds(rb, ROWS)
            top = sbuf[rows, :LANES]
            for c in range(1, KEY_COLS):
                top = jnp.maximum(top, sbuf[rows, c * LANES:(c + 1) * LANES])
            top = jnp.max(top, axis=1, keepdims=True)
            total = jnp.zeros((ROWS, LANES), jnp.float32)
            for c in range(KEY_COLS):
                e = jnp.exp(sbuf[rows, c * LANES:(c + 1) * LANES] - top)
                sbuf[rows, c * LANES:(c + 1) * LANES] = e
                total = total + e
            inv = 1.0 / jnp.sum(total, axis=1, keepdims=True)
            for c in range(KEY_COLS):
                wbuf[t, rows, c * LANES:(c + 1) * LANES] = (
                    sbuf[rows, c * LANES:(c + 1) * LANES] * inv
                ).astype(jnp.bfloat16)

    def weigh_group(gi, carry):
        lax.fori_loop(0, 4, lambda i, c: (weigh_tile(gi * 4 + i), c)[1], 0)
        gx = gi + (gi // 2) * (1 - 2 * lax.rem(gi, 2))
        for hop in (0, 1):
            z_copy(1, hop, gi, gx).wait_recv()
            z_copy(1, hop + 2, gi, gx).start()
        return carry

    lax.fori_loop(0, 4, weigh_group, 0)
    for gi in range(4):
        for hop in (2, 3):
            z_copy(1, hop, gi, GX[gi]).wait_recv()

    def o_copy(t):
        return remote(obuf.at[t], orecv.at[me], o_send.at[t], o_recv.at[me], (view, t))

    def sum_tile(d, carry):
        t = lax.rem(me + 1 + d, toks)
        parts = [vbuf[t]]
        for j in range(NB):
            parts += [vbuf[tile_at(j, t, i)] for i in range(BAND)]
        acc = jnp.dot(wbuf[t], jnp.concatenate(parts, axis=0), preferred_element_type=jnp.float32)
        obuf[t] = jnp.where(low, acc[:TILE], acc[TILE:]).astype(jnp.bfloat16)

        @pl.when(t != me)
        def _():
            o_copy(t).start()

        return carry

    lax.fori_loop(0, 16, sum_tile, 0)
    orecv[me] = obuf[me]

    for d in range(1, 16):
        src = lax.rem(me + toks - d, toks)
        remote(obuf.at[0], orecv.at[src], o_send.at[0], o_recv.at[src], (view, src)).wait_recv()
    for s in range(2):
        role = first_slot if s == 0 else 1 - first_slot
        for p in range(8):
            ost[s, :, p * LANES:(p + 1) * LANES] = orecv[p * 2 + role]
    pltpu.make_async_copy(ost, out_ref.at[0], out_sem).start()

    for d in range(1, 16):
        peer = lax.rem(me + d, toks)
        for a in range(3):
            a2a_copy(a, peer).wait_send()
        o_copy(peer).wait_send()
    for a in range(2):
        for hop in range(4):
            for gi in range(4):
                z_copy(a, hop, gi, GX[gi]).wait_send()
    pltpu.make_async_copy(ost, out_ref.at[0], out_sem).wait()


def local(queries, keys, values, tile_mask, offsets, branch_slots):
    bf16 = jnp.bfloat16
    smem = pl.BlockSpec(memory_space=pltpu.SMEM)
    hbm = pl.BlockSpec(memory_space=pl.ANY)
    dma = pltpu.SemaphoreType.DMA
    return pl.pallas_call(
        attend_kernel,
        out_shape=jax.ShapeDtypeStruct(queries.shape, bf16),
        in_specs=[smem, smem, smem, hbm, hbm, hbm],
        out_specs=hbm,
        scratch_shapes=[
            pltpu.VMEM((2, TILE, 1024), bf16),
            pltpu.VMEM((2, TILE, 1024), bf16),
            pltpu.VMEM((2, TILE, 1024), bf16),
            pltpu.VMEM((3, 16, TILE, LANES), bf16),
            pltpu.VMEM((16, TILE, LANES), bf16),
            pltpu.VMEM((80, TILE, LANES), bf16),
            pltpu.VMEM((80, TILE, LANES), bf16),
            pltpu.VMEM((2 * TILE, KEY_COLS * LANES), jnp.float32),
            pltpu.VMEM((16, 2 * TILE, KEY_COLS * LANES), bf16),
            pltpu.VMEM((16, TILE, LANES), bf16),
            pltpu.VMEM((16, TILE, LANES), bf16),
            pltpu.VMEM((2, TILE, 1024), bf16),
            pltpu.SMEM((NB, 16), jnp.int32),
            pltpu.SMEM((NB, 16), jnp.int32),
            dma((3,)),
            dma((3, 16)),
            dma((3, 16)),
            dma((2, 4, 4)),
            dma((2, 4, 4)),
            dma((16,)),
            dma((16,)),
            dma(()),
        ],
        compiler_params=pltpu.CompilerParams(
            collective_id=0, has_side_effects=True, vmem_limit_bytes=48 * 1024 * 1024
        ),
        cost_estimate=pl.CostEstimate(flops=3_500_000_000, bytes_accessed=2 << 20, transcendentals=7_000_000),
    )(tile_mask, offsets, branch_slots, queries, keys, values)


def solution(mesh):
    in_specs = (
        P("view", None, "tok", None),
        P("view", None, "tok", None),
        P("view", None, "tok", None),
        P("view", None, None, None),
        P("view", None),
        P(),
    )
    out_specs = P("view", None, "tok", None)
    return jax.shard_map(local, mesh=mesh, in_specs=in_specs, out_specs=out_specs, check_vma=False)
```

```python
import jax
import jax.numpy as jnp
from jax import lax
from jax.experimental import pallas as pl
from jax.experimental.pallas import tpu as pltpu
from jax.sharding import PartitionSpec as P

MESH = pl.DeviceIdType.MESH
TILE = 128
LANES = 128
HD = 64
BAND = 6
NB = 2
KEY_COLS = 1 + NB * BAND
NEG_SCORE = -1e30
XS = 4
ROWS = 64
GX = (0, 1, 3, 2)


def attend_kernel(
    mask_ref, off_ref, slot_ref, q_ref, k_ref, v_ref, out_ref,
    raw_k, raw_v, raw_q, stage, qbuf, kbuf, vbuf, sbuf, wbuf, obuf, orecv, ost, start_s, count_s,
    in_sem, a_send, a_recv, z_send, z_recv, o_send, o_recv, out_sem,
):
    views = lax.axis_size("view")
    toks = lax.axis_size("tok")
    group = toks // XS
    view = lax.axis_index("view")
    me = lax.axis_index("tok")
    right = lax.rem(view + 1, views)
    left = lax.rem(view + views - 1, views)
    my_x = me // group
    my_r = lax.rem(me, group)
    half = views // 2
    upper = view // half

    def flip(tok, by):
        return tok + by * (2 - 4 * lax.rem(tok // 2, 2))

    def unit_of(tok):
        return flip(tok, upper)

    right_dev = (right, flip(me, lax.rem(upper + right // half, 2)))
    left_dev = (left, flip(me, lax.rem(upper + left // half, 2)))
    bufs = (kbuf, vbuf, qbuf)
    raws = (raw_k, raw_v, raw_q)

    def remote(src, dst, send, recv, dev):
        return pltpu.make_async_remote_copy(
            src_ref=src, dst_ref=dst, send_sem=send, recv_sem=recv, device_id=dev, device_id_type=MESH
        )

    def in_copy(a):
        return pltpu.make_async_copy((k_ref, v_ref, q_ref)[a].at[0], raws[a], in_sem.at[a])

    for a in range(3):
        in_copy(a).start()

    barrier = pltpu.get_barrier_semaphore()
    for d in range(1, 16):
        pl.semaphore_signal(barrier, inc=1, device_id=(view, lax.rem(me + d, toks)), device_id_type=MESH)
    for to in (right_dev, left_dev):
        pl.semaphore_signal(barrier, inc=1, device_id=to, device_id_type=MESH)

    first_slot = slot_ref[view, 0]

    def stage_array(a):
        in_copy(a).wait()
        for b in range(2):
            slot = first_slot if b == 0 else 1 - first_slot
            for p in range(8):
                stage[a, p * 2 + b] = raws[a][slot, :, p * LANES:(p + 1) * LANES]
        bufs[a][me] = stage[a, unit_of(me)]

    def a2a_copy(a, dest):
        return remote(stage.at[a, unit_of(dest)], bufs[a].at[me], a_send.at[a, dest], a_recv.at[a, me], (view, dest))

    def a2a_send(a):
        for gx in GX:
            for r in range(4):
                if (gx, r) != (0, 0):
                    dest = lax.rem(my_x + gx, XS) * group + lax.rem(my_r + r, group)
                    a2a_copy(a, dest).start()

    def a2a_wait(a, gx):
        for r in range(4):
            if (gx, r) != (0, 0):
                src = lax.rem(my_x + XS - gx, XS) * group + lax.rem(my_r + group - r, group)
                remote(stage.at[a, 0], bufs[a].at[src], a_send.at[a, 0], a_recv.at[a, src], (view, src)).wait_recv()

    def z_copy(a, hop, gi, gx):
        start = lax.rem(my_x + XS - gx, XS) * group
        src_set, dst_set, dev = ((0, 1, right_dev), (0, 2, left_dev), (1, 3, right_dev), (2, 4, left_dev))[hop]
        return remote(
            bufs[a].at[pl.ds(src_set * toks + start, 4)],
            bufs[a].at[pl.ds(dst_set * toks + start, 4)],
            z_send.at[a, hop, gi], z_recv.at[a, hop, gi], dev,
        )

    stage_array(0)
    pl.semaphore_wait(barrier, 17)
    a2a_send(0)
    a2a_wait(0, GX[0])
    for hop in (0, 1):
        z_copy(0, hop, 0, GX[0]).start()
    stage_array(1)
    a2a_send(1)
    a2a_wait(0, GX[1])
    for hop in (0, 1):
        z_copy(0, hop, 1, GX[1]).start()
    stage_array(2)
    a2a_send(2)
    for gi in (2, 3):
        a2a_wait(0, GX[gi])
        for hop in (0, 1):
            z_copy(0, hop, gi, GX[gi]).start()
    for gi in range(4):
        for hop in (0, 1):
            z_copy(0, hop, gi, GX[gi]).wait_recv()
            z_copy(0, hop + 2, gi, GX[gi]).start()
    for gi in range(4):
        a2a_wait(1, GX[gi])
        for hop in (0, 1):
            z_copy(1, hop, gi, GX[gi]).start()

    for j in range(NB):
        def count_row(t, carry, j=j):
            first = jnp.int32(0)
            total = jnp.int32(0)
            before = mask_ref[0, j, t, 15]
            for k in range(16):
                here = mask_ref[0, j, t, k]
                total = total + here
                first = first + jnp.where((here == 1) & (before == 0), k, 0)
                before = here
            start_s[j, t] = first
            count_s[j, t] = total
            return carry
        lax.fori_loop(0, 16, count_row, 0)

    for gx in GX:
        a2a_wait(2, gx)
    for gi in range(4):
        for hop in (2, 3):
            z_copy(0, hop, gi, GX[gi]).wait_recv()

    sets = []
    for j in range(NB):
        off = off_ref[0, j]
        sets.append(jnp.where(off == -1, 1, jnp.where(off == 1, 2, jnp.where(off == -2, 3, 4))) * toks)
    low = lax.broadcasted_iota(jnp.int32, (TILE, LANES), 1) < HD

    def tile_at(j, t, i):
        return sets[j] + lax.rem(start_s[j, t] + i, 16)

    def dot_t(x, y):
        return lax.dot_general(x, y, (((1,), (1,)), ((), ())), preferred_element_type=jnp.float32)

    def weigh_tile(t):
        q = qbuf[t] * jnp.bfloat16(0.125)
        zero = jnp.zeros_like(q)
        both = jnp.concatenate([jnp.where(low, q, zero), jnp.where(low, zero, q)], axis=0)
        sbuf[:, :LANES] = dot_t(both, kbuf[t])
        for j in range(NB):
            for i in range(0, BAND, 2):
                keys = jnp.concatenate([kbuf[tile_at(j, t, i)], kbuf[tile_at(j, t, i + 1)]], axis=0)
                s = dot_t(both, keys)
                for h in range(2):
                    bias = jnp.where(i + h < count_s[j, t], jnp.float32(0), jnp.float32(NEG_SCORE))
                    c = 1 + j * BAND + i + h
                    sbuf[:, c * LANES:(c + 1) * LANES] = s[:, h * LANES:(h + 1) * LANES] + bias
        for rb in range(0, 2 * TILE, ROWS):
            rows = pl.ds(rb, ROWS)
            top = sbuf[rows, :LANES]
            for c in range(1, KEY_COLS):
                top = jnp.maximum(top, sbuf[rows, c * LANES:(c + 1) * LANES])
            top = jnp.max(top, axis=1, keepdims=True)
            total = jnp.zeros((ROWS, LANES), jnp.float32)
            for c in range(KEY_COLS):
                e = jnp.exp(sbuf[rows, c * LANES:(c + 1) * LANES] - top)
                sbuf[rows, c * LANES:(c + 1) * LANES] = e
                total = total + e
            inv = 1.0 / jnp.sum(total, axis=1, keepdims=True)
            for c in range(KEY_COLS):
                wbuf[t, rows, c * LANES:(c + 1) * LANES] = (
                    sbuf[rows, c * LANES:(c + 1) * LANES] * inv
                ).astype(jnp.bfloat16)

    def weigh_group(gi, carry):
        lax.fori_loop(0, 4, lambda i, c: (weigh_tile(gi * 4 + i), c)[1], 0)
        gx = gi + (gi // 2) * (1 - 2 * lax.rem(gi, 2))
        for hop in (0, 1):
            z_copy(1, hop, gi, gx).wait_recv()
            z_copy(1, hop + 2, gi, gx).start()
        return carry

    lax.fori_loop(0, 4, weigh_group, 0)
    for gi in range(4):
        for hop in (2, 3):
            z_copy(1, hop, gi, GX[gi]).wait_recv()

    def o_copy(t):
        return remote(obuf.at[t], orecv.at[unit_of(me)], o_send.at[t], o_recv.at[me], (view, t))

    def sum_tile(d, carry):
        t = lax.rem(me + 1 + d, toks)
        parts = [vbuf[t]]
        for j in range(NB):
            parts += [vbuf[tile_at(j, t, i)] for i in range(BAND)]
        acc = jnp.dot(wbuf[t], jnp.concatenate(parts, axis=0), preferred_element_type=jnp.float32)
        obuf[t] = jnp.where(low, acc[:TILE], acc[TILE:]).astype(jnp.bfloat16)

        @pl.when(t != me)
        def _():
            o_copy(t).start()

        return carry

    lax.fori_loop(0, 16, sum_tile, 0)
    orecv[unit_of(me)] = obuf[me]

    for d in range(1, 16):
        src = lax.rem(me + toks - d, toks)
        remote(obuf.at[0], orecv.at[unit_of(src)], o_send.at[0], o_recv.at[src], (view, src)).wait_recv()
    for s in range(2):
        role = first_slot if s == 0 else 1 - first_slot
        for p in range(8):
            ost[s, :, p * LANES:(p + 1) * LANES] = orecv[p * 2 + role]
    pltpu.make_async_copy(ost, out_ref.at[0], out_sem).start()

    for d in range(1, 16):
        peer = lax.rem(me + d, toks)
        for a in range(3):
            a2a_copy(a, peer).wait_send()
        o_copy(peer).wait_send()
    for a in range(2):
        for hop in range(4):
            for gi in range(4):
                z_copy(a, hop, gi, GX[gi]).wait_send()
    pltpu.make_async_copy(ost, out_ref.at[0], out_sem).wait()


def local(queries, keys, values, tile_mask, offsets, branch_slots):
    bf16 = jnp.bfloat16
    smem = pl.BlockSpec(memory_space=pltpu.SMEM)
    hbm = pl.BlockSpec(memory_space=pl.ANY)
    dma = pltpu.SemaphoreType.DMA
    return pl.pallas_call(
        attend_kernel,
        out_shape=jax.ShapeDtypeStruct(queries.shape, bf16),
        in_specs=[smem, smem, smem, hbm, hbm, hbm],
        out_specs=hbm,
        scratch_shapes=[
            pltpu.VMEM((2, TILE, 1024), bf16),
            pltpu.VMEM((2, TILE, 1024), bf16),
            pltpu.VMEM((2, TILE, 1024), bf16),
            pltpu.VMEM((3, 16, TILE, LANES), bf16),
            pltpu.VMEM((16, TILE, LANES), bf16),
            pltpu.VMEM((80, TILE, LANES), bf16),
            pltpu.VMEM((80, TILE, LANES), bf16),
            pltpu.VMEM((2 * TILE, KEY_COLS * LANES), jnp.float32),
            pltpu.VMEM((16, 2 * TILE, KEY_COLS * LANES), bf16),
            pltpu.VMEM((16, TILE, LANES), bf16),
            pltpu.VMEM((16, TILE, LANES), bf16),
            pltpu.VMEM((2, TILE, 1024), bf16),
            pltpu.SMEM((NB, 16), jnp.int32),
            pltpu.SMEM((NB, 16), jnp.int32),
            dma((3,)),
            dma((3, 16)),
            dma((3, 16)),
            dma((2, 4, 4)),
            dma((2, 4, 4)),
            dma((16,)),
            dma((16,)),
            dma(()),
        ],
        compiler_params=pltpu.CompilerParams(
            collective_id=0, has_side_effects=True, vmem_limit_bytes=48 * 1024 * 1024
        ),
        cost_estimate=pl.CostEstimate(flops=3_500_000_000, bytes_accessed=2 << 20, transcendentals=7_000_000),
    )(tile_mask, offsets, branch_slots, queries, keys, values)


def solution(mesh):
    in_specs = (
        P("view", None, "tok", None),
        P("view", None, "tok", None),
        P("view", None, "tok", None),
        P("view", None, None, None),
        P("view", None),
        P(),
    )
    out_specs = P("view", None, "tok", None)
    return jax.shard_map(local, mesh=mesh, in_specs=in_specs, out_specs=out_specs, check_vma=False)
```

```python
import jax
import jax.numpy as jnp
from jax import lax
from jax.experimental import pallas as pl
from jax.experimental.pallas import tpu as pltpu
from jax.sharding import PartitionSpec as P

MESH = pl.DeviceIdType.MESH
TILE = 128
LANES = 128
HD = 64
BAND = 6
NB = 2
KEY_COLS = 1 + NB * BAND
NEG_SCORE = -1e30
VMEM_BYTES = 63 * 1024 * 1024
XS = 4
ROWS = 64
LOW_STEP = 1
HIGH_STEP = 11
GX = (0, 1, 3, 2)


def attend_kernel(
    mask_ref, off_ref, slot_ref, q_ref, k_ref, v_ref, out_ref,
    raw_k, raw_v, raw_q, stage_k, stage_v, stage_q, qbuf, kbuf, vown, vlow, vhigh, vun_low, vun_high, sbuf, wbuf,
    obuf, orecv, start_s, count_s,
    in_sem, a_send, a_recv, z_send, z_recv, o_send, o_recv,
):
    views = lax.axis_size("view")
    toks = lax.axis_size("tok")
    group = toks // XS
    view = lax.axis_index("view")
    me = lax.axis_index("tok")
    right = lax.rem(view + 1, views)
    left = lax.rem(view + views - 1, views)
    my_x = me // group
    my_r = lax.rem(me, group)
    half = views // 2
    upper = view // half

    def flip(tok, by):
        return tok + by * (2 - 4 * lax.rem(tok // 2, 2))

    def unit_of(tok):
        return flip(tok, upper)

    right_dev = (right, flip(me, lax.rem(upper + right // half, 2)))
    left_dev = (left, flip(me, lax.rem(upper + left // half, 2)))
    raws = (raw_k, raw_v, raw_q)
    stages = (stage_k, stage_v, stage_q)
    bufs = (kbuf, vown, qbuf)

    def remote(src, dst, send, recv, dev):
        return pltpu.make_async_remote_copy(
            src_ref=src, dst_ref=dst, send_sem=send, recv_sem=recv, device_id=dev, device_id_type=MESH
        )

    def in_copy(a):
        return pltpu.make_async_copy((k_ref, v_ref, q_ref)[a].at[0], raws[a], in_sem.at[a])

    for a in range(3):
        in_copy(a).start()

    barrier = pltpu.get_barrier_semaphore()
    for to in (right_dev, left_dev):
        pl.semaphore_signal(barrier, inc=1, device_id=to, device_id_type=MESH)
    for d in range(1, 16):
        pl.semaphore_signal(barrier, inc=1, device_id=(view, lax.rem(me + d, toks)), device_id_type=MESH)

    first_slot = slot_ref[0, view]

    def swap_halves(x, y):
        return (
            jnp.concatenate([x[:, :HD], y[:, :HD]], axis=1),
            jnp.concatenate([x[:, HD:], y[:, HD:]], axis=1),
        )

    def stage_array(a):
        in_copy(a).wait()
        for b in range(2):
            slot = first_slot if b == 0 else 1 - first_slot
            for p in range(8):
                tile = raws[a][slot, :, p * LANES:(p + 1) * LANES]
                if a == 1:
                    low_head, high_head = swap_halves(tile[:HD], tile[HD:])
                    stage_v[p * 2 + b, 0] = low_head
                    stage_v[p * 2 + b, 1] = high_head
                else:
                    stages[a][p * 2 + b] = tile
        bufs[a][me] = stages[a][unit_of(me)]

    def a2a_copy(a, dest):
        return remote(stages[a].at[unit_of(dest)], bufs[a].at[me], a_send.at[a, dest], a_recv.at[a, me], (view, dest))

    def a2a_send(a, columns=GX):
        for gx in columns:
            for r in range(4):
                if (gx, r) != (0, 0):
                    dest = lax.rem(my_x + gx, XS) * group + lax.rem(my_r + r, group)
                    a2a_copy(a, dest).start()

    def a2a_wait(a, gx):
        for r in range(4):
            if (gx, r) != (0, 0):
                src = lax.rem(my_x + XS - gx, XS) * group + lax.rem(my_r + group - r, group)
                remote(stages[a].at[0], bufs[a].at[src], a_send.at[a, 0], a_recv.at[a, src], (view, src)).wait_recv()

    def z_copy(a, hop, gi, gx):
        start = lax.rem(my_x + XS - gx, XS) * group
        src_set, dst_set, dev = ((0, 1, right_dev), (0, 2, left_dev), (1, 3, right_dev), (2, 4, left_dev))[hop]
        if a == 0:
            src = kbuf.at[pl.ds(src_set * toks + start, 4)]
            dst = kbuf.at[pl.ds(dst_set * toks + start, 4)]
        else:
            buf = (vlow, vhigh)[a - 1]
            if hop < 2:
                src = vown.at[pl.ds(start, 4), a - 1]
            else:
                src = buf.at[pl.ds((src_set - 1) * toks + start, 4)]
            dst = buf.at[pl.ds((dst_set - 1) * toks + start, 4)]
        return remote(src, dst, z_send.at[a, hop, gi], z_recv.at[a, hop, gi], dev)

    def send_own(a, gi, gx):
        for hop in (0, 1):
            z_copy(a, hop, gi, gx).start()

    def send_on(a, gi, gx):
        for hop in (0, 1):
            z_copy(a, hop, gi, gx).wait_recv()
            z_copy(a, hop + 2, gi, gx).start()

    def wait_far(a):
        for gi in range(4):
            for hop in (2, 3):
                z_copy(a, hop, gi, GX[gi]).wait_recv()

    stage_array(0)
    pl.semaphore_wait(barrier, 17)
    a2a_send(0, (0,))
    a2a_send(0, (1, 3))
    a2a_wait(0, 0)
    send_own(0, 0, 0)
    a2a_send(0, (2,))
    stage_array(1)
    for gi in (1, 2):
        a2a_wait(0, GX[gi])
        send_own(0, gi, GX[gi])
    stage_array(2)
    a2a_send(1)
    a2a_send(2)
    a2a_wait(0, GX[3])
    send_own(0, 3, GX[3])
    for gi in range(4):
        send_on(0, gi, GX[gi])
    for gi in range(4):
        a2a_wait(1, GX[gi])
        send_own(1, gi, GX[gi])

    for j in range(NB):
        def count_row(t, carry, j=j):
            first = jnp.int32(0)
            total = jnp.int32(0)
            before = mask_ref[0, j, t, 15]
            for k in range(16):
                here = mask_ref[0, j, t, k]
                total = total + here
                first = first + jnp.where((here == 1) & (before == 0), k, 0)
                before = here
            start_s[j, t] = first
            count_s[j, t] = total
            return carry
        lax.fori_loop(0, 16, count_row, 0)

    for gx in GX:
        a2a_wait(2, gx)
    wait_far(0)

    sets = []
    for j in range(NB):
        off = off_ref[0, j]
        sets.append(jnp.where(off == -1, 1, jnp.where(off == 1, 2, jnp.where(off == -2, 3, 4))) * toks)
    low = lax.broadcasted_iota(jnp.int32, (TILE, LANES), 1) < HD

    def paired(j, t, i):
        return lax.rem(start_s[j, t] + i, 16)

    def dot_t(x, y):
        return lax.dot_general(x, y, (((1,), (1,)), ((), ())), preferred_element_type=jnp.float32)

    def weigh_tile(t):
        q = qbuf[t] * jnp.bfloat16(0.125)
        zero = jnp.zeros_like(q)
        both = jnp.concatenate([jnp.where(low, q, zero), jnp.where(low, zero, q)], axis=0)
        sbuf[:, :LANES] = dot_t(both, kbuf[t])
        for j in range(NB):
            for i in range(0, BAND, 2):
                keys = jnp.concatenate(
                    [kbuf[sets[j] + paired(j, t, i)], kbuf[sets[j] + paired(j, t, i + 1)]], axis=0
                )
                s = dot_t(both, keys)
                for h in range(2):
                    bias = jnp.where(i + h < count_s[j, t], jnp.float32(0), jnp.float32(NEG_SCORE))
                    c = 1 + j * BAND + i + h
                    sbuf[:, c * LANES:(c + 1) * LANES] = s[:, h * LANES:(h + 1) * LANES] + bias
        for rb in range(0, 2 * TILE, ROWS):
            rows = pl.ds(rb, ROWS)
            top = sbuf[rows, :LANES]
            for c in range(1, KEY_COLS):
                top = jnp.maximum(top, sbuf[rows, c * LANES:(c + 1) * LANES])
            top = jnp.max(top, axis=1, keepdims=True)
            total = jnp.zeros((ROWS, LANES), jnp.float32)
            for c in range(KEY_COLS):
                e = jnp.exp(sbuf[rows, c * LANES:(c + 1) * LANES] - top)
                sbuf[rows, c * LANES:(c + 1) * LANES] = e
                total = total + e
            inv = 1.0 / jnp.sum(total, axis=1, keepdims=True)
            for c in range(KEY_COLS):
                wbuf[t, rows, c * LANES:(c + 1) * LANES] = (
                    sbuf[rows, c * LANES:(c + 1) * LANES] * inv
                ).astype(jnp.bfloat16)

    def gx_of(gi):
        return gi + (gi // 2) * (1 - 2 * lax.rem(gi, 2))

    def weigh_step(t, carry):
        weigh_tile(t)

        @pl.when((t >= LOW_STEP) & (t < LOW_STEP + 4))
        def _():
            gi = t - LOW_STEP
            send_on(1, gi, gx_of(gi))
            send_own(2, gi, gx_of(gi))

        @pl.when((t >= HIGH_STEP) & (t < HIGH_STEP + 4))
        def _():
            gi = t - HIGH_STEP
            send_on(2, gi, gx_of(gi))

        return carry

    lax.fori_loop(0, 16, weigh_step, 0)

    def o_copy(h, t):
        return remote(obuf.at[h, t], orecv.at[h, unit_of(me)], o_send.at[h, t], o_recv.at[h, me], (view, t))

    for h in range(2):
        wait_far(1 + h)
        buf = (vlow, vhigh)[h]
        vun = (vun_low, vun_high)[h]

        def unpack(t, carry, h=h, buf=buf, vun=vun):
            for n in range(1 + NB):
                pack = vown[t, h] if n == 0 else buf[sets[n - 1] - toks + t]
                vun[n * 16 + t, :HD] = pack
                vun[n * 16 + t, HD:] = jnp.concatenate([pack[:, HD:], pack[:, :HD]], axis=1)
            return carry

        lax.fori_loop(0, 16, unpack, 0)

        def sum_tiles(d, carry, h=h, vun=vun):
            ts = [lax.rem(me + 1 + 4 * d + n, toks) for n in range(4)]
            for t in ts:
                parts = [vun[t]]
                for j in range(NB):
                    parts += [vun[16 * (1 + j) + paired(j, t, i)] for i in range(BAND)]
                acc = jnp.dot(
                    wbuf[t, h * TILE:(h + 1) * TILE], jnp.concatenate(parts, axis=0),
                    preferred_element_type=jnp.float32,
                )
                obuf[h, t] = jnp.concatenate([acc[:HD, :HD], acc[HD:, :HD]], axis=1).astype(jnp.bfloat16)
            for t in ts:
                @pl.when(t != me)
                def _(t=t):
                    o_copy(h, t).start()

            return carry

        lax.fori_loop(0, 4, sum_tiles, 0)
        orecv[h, unit_of(me)] = obuf[h, me]

    for h in range(2):
        for d in range(1, 16):
            src = lax.rem(me + toks - d, toks)
            remote(obuf.at[0, 0], orecv.at[h, unit_of(src)], o_send.at[h, 0], o_recv.at[h, src], (view, src)).wait_recv()
    for s in range(2):
        role = first_slot if s == 0 else 1 - first_slot
        for p in range(8):
            upper_rows, lower_rows = swap_halves(orecv[0, p * 2 + role], orecv[1, p * 2 + role])
            out_ref[0, s, :HD, p * LANES:(p + 1) * LANES] = upper_rows
            out_ref[0, s, HD:, p * LANES:(p + 1) * LANES] = lower_rows

    for d in range(1, 16):
        peer = lax.rem(me + d, toks)
        for a in range(3):
            a2a_copy(a, peer).wait_send()
        for h in range(2):
            o_copy(h, peer).wait_send()
    for a in range(3):
        for hop in range(4):
            for gi in range(4):
                z_copy(a, hop, gi, GX[gi]).wait_send()


def local(queries, keys, values, tile_mask, offsets, branch_slots):
    bf16 = jnp.bfloat16
    smem = pl.BlockSpec(memory_space=pltpu.SMEM)
    hbm = pl.BlockSpec(memory_space=pl.ANY)
    dma = pltpu.SemaphoreType.DMA
    return pl.pallas_call(
        attend_kernel,
        out_shape=jax.ShapeDtypeStruct(queries.shape, bf16),
        in_specs=[smem, smem, smem, hbm, hbm, hbm],
        out_specs=pl.BlockSpec(memory_space=pltpu.VMEM),
        scratch_shapes=[
            pltpu.VMEM((2, TILE, 1024), bf16),
            pltpu.VMEM((2, TILE, 1024), bf16),
            pltpu.VMEM((2, TILE, 1024), bf16),
            pltpu.VMEM((16, TILE, LANES), bf16),
            pltpu.VMEM((16, 2, HD, LANES), bf16),
            pltpu.VMEM((16, TILE, LANES), bf16),
            pltpu.VMEM((16, TILE, LANES), bf16),
            pltpu.VMEM((80, TILE, LANES), bf16),
            pltpu.VMEM((16, 2, HD, LANES), bf16),
            pltpu.VMEM((64, HD, LANES), bf16),
            pltpu.VMEM((64, HD, LANES), bf16),
            pltpu.VMEM((48, TILE, LANES), bf16),
            pltpu.VMEM((48, TILE, LANES), bf16),
            pltpu.VMEM((2 * TILE, KEY_COLS * LANES), jnp.float32),
            pltpu.VMEM((16, 2 * TILE, KEY_COLS * LANES), bf16),
            pltpu.VMEM((2, 16, HD, LANES), bf16),
            pltpu.VMEM((2, 16, HD, LANES), bf16),
            pltpu.SMEM((NB, 16), jnp.int32),
            pltpu.SMEM((NB, 16), jnp.int32),
            dma((3,)),
            dma((3, 16)),
            dma((3, 16)),
            dma((3, 4, 4)),
            dma((3, 4, 4)),
            dma((2, 16)),
            dma((2, 16)),
        ],
        compiler_params=pltpu.CompilerParams(
            collective_id=0, has_side_effects=True, vmem_limit_bytes=VMEM_BYTES
        ),
        cost_estimate=pl.CostEstimate(flops=3_500_000_000, bytes_accessed=2 << 20, transcendentals=7_000_000),
    )(tile_mask, offsets, branch_slots.T, queries, keys, values)


def solution(mesh):
    in_specs = (
        P("view", None, "tok", None),
        P("view", None, "tok", None),
        P("view", None, "tok", None),
        P("view", None, None, None),
        P("view", None),
        P(),
    )
    out_specs = P("view", None, "tok", None)
    return jax.shard_map(local, mesh=mesh, in_specs=in_specs, out_specs=out_specs, check_vma=False)
```

```python
import jax
import jax.numpy as jnp
from jax import lax
from jax.experimental import pallas as pl
from jax.experimental.pallas import tpu as pltpu
from jax.sharding import PartitionSpec as P

MESH = pl.DeviceIdType.MESH
TILE = 128
LANES = 128
HD = 64
BAND = 6
NB = 2
KEY_COLS = 1 + NB * BAND
NEG_SCORE = -1e30
VMEM_BYTES = 63 * 1024 * 1024
XS = 4
ROWS = 64
LOW_STEP = 1
HIGH_STEP = 11
GX = (0, 1, 3, 2)


def attend_kernel(
    mask_in, off_in, slot_in, q_ref, k_ref, v_ref, out_ref,
    mask_ref, off_ref, slot_ref,
    raw_k, raw_v, raw_q, stage_k, stage_v, stage_q, qbuf, kbuf, vown, vlow, vhigh, own_sum, sbuf, wbuf,
    obuf, orecv, start_s, count_s,
    in_sem, a_send, a_recv, z_send, z_recv, o_send, o_recv,
):
    views = lax.axis_size("view")
    toks = lax.axis_size("tok")
    group = toks // XS
    view = lax.axis_index("view")
    me = lax.axis_index("tok")
    right = lax.rem(view + 1, views)
    left = lax.rem(view + views - 1, views)
    my_x = me // group
    my_r = lax.rem(me, group)
    half = views // 2
    upper = view // half

    def flip(tok, by):
        return tok + by * (2 - 4 * lax.rem(tok // 2, 2))

    def unit_of(tok):
        return flip(tok, upper)

    right_dev = (right, flip(me, lax.rem(upper + right // half, 2)))
    left_dev = (left, flip(me, lax.rem(upper + left // half, 2)))
    raws = (raw_k, raw_v, raw_q)
    stages = (stage_k, stage_v, stage_q)
    bufs = (kbuf, vown, qbuf)

    def remote(src, dst, send, recv, dev):
        return pltpu.make_async_remote_copy(
            src_ref=src, dst_ref=dst, send_sem=send, recv_sem=recv, device_id=dev, device_id_type=MESH
        )

    def in_copy(a):
        return pltpu.make_async_copy((k_ref, v_ref, q_ref)[a].at[0], raws[a], in_sem.at[a])

    tables = [
        pltpu.make_async_copy(src, dst, in_sem.at[3 + n])
        for n, (src, dst) in enumerate(((slot_in, slot_ref), (off_in, off_ref), (mask_in, mask_ref)))
    ]
    tables[0].start()
    for a in range(3):
        in_copy(a).start()
    for table in tables[1:]:
        table.start()

    barrier = pltpu.get_barrier_semaphore()
    for to in (right_dev, left_dev):
        pl.semaphore_signal(barrier, inc=1, device_id=to, device_id_type=MESH)
    for d in range(1, 16):
        pl.semaphore_signal(barrier, inc=1, device_id=(view, lax.rem(me + d, toks)), device_id_type=MESH)

    tables[0].wait()
    first_slot = slot_ref[0, view]

    def swap_halves(x, y):
        return (
            jnp.concatenate([x[:, :HD], y[:, :HD]], axis=1),
            jnp.concatenate([x[:, HD:], y[:, HD:]], axis=1),
        )

    def stage_array(a):
        in_copy(a).wait()
        for b in range(2):
            slot = first_slot if b == 0 else 1 - first_slot
            for p in range(8):
                tile = raws[a][slot, :, p * LANES:(p + 1) * LANES]
                if a == 1:
                    low_head, high_head = swap_halves(tile[:HD], tile[HD:])
                    stage_v[p * 2 + b, 0] = low_head
                    stage_v[p * 2 + b, 1] = high_head
                else:
                    stages[a][p * 2 + b] = tile
        bufs[a][me] = stages[a][unit_of(me)]

    def a2a_copy(a, dest):
        return remote(stages[a].at[unit_of(dest)], bufs[a].at[me], a_send.at[a, dest], a_recv.at[a, me], (view, dest))

    def mate(r, n):
        other = r + 1 - 2 * lax.rem(r, 2) if n % 2 else r
        return lax.rem(other + 2, group) if n >= 2 else other

    def a2a_send(a, columns=GX):
        for gx in columns:
            for n in range(4):
                if (gx, n) != (0, 0):
                    a2a_copy(a, lax.rem(my_x + gx, XS) * group + mate(my_r, n)).start()

    def a2a_wait(a, gx, mates=range(4)):
        for n in mates:
            if (gx, n) != (0, 0):
                src = lax.rem(my_x + XS - gx, XS) * group + mate(my_r, n)
                remote(stages[a].at[0], bufs[a].at[src], a_send.at[a, 0], a_recv.at[a, src], (view, src)).wait_recv()

    def z_copy(a, hop, gi, gx):
        start = lax.rem(my_x + XS - gx, XS) * group
        src_set, dst_set, dev = ((0, 1, right_dev), (0, 2, left_dev), (1, 3, right_dev), (2, 4, left_dev))[hop]
        if a == 0:
            src = kbuf.at[pl.ds(src_set * toks + start, 4)]
            dst = kbuf.at[pl.ds(dst_set * toks + start, 4)]
        else:
            buf = (vlow, vhigh)[a - 1]
            if hop < 2:
                src = vown.at[pl.ds(start, 4), a - 1]
            else:
                src = buf.at[pl.ds((src_set - 1) * toks + start, 4)]
            dst = buf.at[pl.ds((dst_set - 1) * toks + start, 4)]
        sem = gi + 3 if a == 0 else gi
        return remote(src, dst, z_send.at[a, hop, sem], z_recv.at[a, hop, sem], dev)

    def unit_place(by):
        return lax.rem(flip(me, lax.rem(upper + lax.rem(view + views + by, views) // half, 2)), group)

    def z_tile(hop, n, origin):
        tile = my_x * group + mate(unit_place(origin), n)
        src_set, dst_set, dev = ((0, 1, right_dev), (0, 2, left_dev), (1, 3, right_dev), (2, 4, left_dev))[hop]
        return remote(
            kbuf.at[src_set * toks + tile], kbuf.at[dst_set * toks + tile],
            z_send.at[0, hop, n], z_recv.at[0, hop, n], dev,
        )

    def send_tile(n):
        for hop in (0, 1):
            z_tile(hop, n, 0).start()

    def send_tile_on(n):
        for hop, origin in ((0, -1), (1, 1)):
            z_tile(hop, n, origin).wait_recv()
            z_tile(hop + 2, n, origin).start()

    def send_own(a, gi, gx):
        for hop in (0, 1):
            z_copy(a, hop, gi, gx).start()

    def send_on(a, gi, gx):
        for hop in (0, 1):
            z_copy(a, hop, gi, gx).wait_recv()
            z_copy(a, hop + 2, gi, gx).start()

    def wait_far(a):
        if a == 0:
            for n in range(4):
                for hop, origin in ((2, -2), (3, 2)):
                    z_tile(hop, n, origin).wait_recv()
        for gi in range(1 if a == 0 else 0, 4):
            for hop in (2, 3):
                z_copy(a, hop, gi, GX[gi]).wait_recv()

    stage_array(0)
    pl.semaphore_wait(barrier, 17)
    send_tile(0)
    a2a_send(0, (0,))
    a2a_send(0, (1, 3))
    for n in range(1, 4):
        a2a_wait(0, 0, (n,))
        send_tile(n)
    a2a_send(0, (2,))
    stage_array(1)
    for gi in (1, 2):
        a2a_wait(0, GX[gi])
        send_own(0, gi, GX[gi])
    stage_array(2)
    a2a_send(1)
    a2a_send(2)
    a2a_wait(0, GX[3])
    send_own(0, 3, GX[3])
    for n in range(4):
        send_tile_on(n)
    for gi in range(1, 4):
        send_on(0, gi, GX[gi])
    for gi in range(4):
        a2a_wait(1, GX[gi])
        send_own(1, gi, GX[gi])

    for table in tables[1:]:
        table.wait()

    for j in range(NB):
        def count_row(t, carry, j=j):
            first = jnp.int32(0)
            total = jnp.int32(0)
            before = mask_ref[0, j, t, 15]
            for k in range(16):
                here = mask_ref[0, j, t, k]
                total = total + here
                first = first + jnp.where((here == 1) & (before == 0), k, 0)
                before = here
            start_s[j, t] = first
            count_s[j, t] = total
            return carry
        lax.fori_loop(0, 16, count_row, 0)

    for gx in GX:
        a2a_wait(2, gx)
    wait_far(0)

    sets = []
    for j in range(NB):
        off = off_ref[0, j]
        sets.append(jnp.where(off == -1, 1, jnp.where(off == 1, 2, jnp.where(off == -2, 3, 4))) * toks)
    low = lax.broadcasted_iota(jnp.int32, (TILE, LANES), 1) < HD
    low_row = lax.broadcasted_iota(jnp.int32, (1, LANES), 1) < HD

    def roll_half(x):
        return jnp.concatenate([x[:, HD:], x[:, :HD]], axis=1)

    def paired(j, t, i):
        return lax.rem(start_s[j, t] + i, 16)

    def dot_t(x, y):
        return lax.dot_general(x, y, (((1,), (1,)), ((), ())), preferred_element_type=jnp.float32)

    def weigh_tile(t):
        q = qbuf[t] * jnp.bfloat16(0.125)
        zero = jnp.zeros_like(q)
        both = jnp.concatenate([jnp.where(low, q, zero), jnp.where(low, zero, q)], axis=0)
        sbuf[:, :LANES] = dot_t(both, kbuf[t])
        for j in range(NB):
            for i in range(0, BAND, 2):
                one, two = kbuf[sets[j] + paired(j, t, i)], kbuf[sets[j] + paired(j, t, i + 1)]
                s = dot_t(both, jnp.concatenate([one[:HD], two[:HD], one[HD:], two[HD:]], axis=0))
                bias = jnp.where(
                    low_row,
                    jnp.where(i < count_s[j, t], jnp.float32(0), jnp.float32(NEG_SCORE)),
                    jnp.where(i + 1 < count_s[j, t], jnp.float32(0), jnp.float32(NEG_SCORE)),
                )
                for h in range(2):
                    c = 1 + h * BAND + (j * BAND + i) // 2
                    sbuf[:, c * LANES:(c + 1) * LANES] = s[:, h * LANES:(h + 1) * LANES] + bias
        for rb in range(0, 2 * TILE, ROWS):
            rows = pl.ds(rb, ROWS)
            top = sbuf[rows, :LANES]
            for c in range(1, KEY_COLS):
                top = jnp.maximum(top, sbuf[rows, c * LANES:(c + 1) * LANES])
            top = jnp.max(top, axis=1, keepdims=True)
            total = jnp.zeros((ROWS, LANES), jnp.float32)
            for c in range(KEY_COLS):
                e = jnp.exp(sbuf[rows, c * LANES:(c + 1) * LANES] - top)
                sbuf[rows, c * LANES:(c + 1) * LANES] = e
                total = total + e
            inv = 1.0 / jnp.sum(total, axis=1, keepdims=True)
            for c in range(KEY_COLS):
                wbuf[t, rows, c * LANES:(c + 1) * LANES] = (
                    sbuf[rows, c * LANES:(c + 1) * LANES] * inv
                ).astype(jnp.bfloat16)
        for h in range(2):
            pack = vown[t, h]
            part = jnp.dot(
                wbuf[t, h * TILE:(h + 1) * TILE, :LANES], jnp.concatenate([pack, roll_half(pack)], axis=0),
                preferred_element_type=jnp.float32,
            )
            own_sum[h, t] = jnp.concatenate([part[:HD, :HD], part[HD:, :HD]], axis=1)

    def gx_of(gi):
        return gi + (gi // 2) * (1 - 2 * lax.rem(gi, 2))

    def weigh_step(t, carry):
        weigh_tile(t)

        @pl.when((t >= LOW_STEP) & (t < LOW_STEP + 4))
        def _():
            gi = t - LOW_STEP
            send_on(1, gi, gx_of(gi))
            send_own(2, gi, gx_of(gi))

        @pl.when((t >= HIGH_STEP) & (t < HIGH_STEP + 4))
        def _():
            gi = t - HIGH_STEP
            send_on(2, gi, gx_of(gi))

        return carry

    lax.fori_loop(0, 16, weigh_step, 0)

    def o_copy(h, t):
        return remote(obuf.at[h, t], orecv.at[h, unit_of(me)], o_send.at[h, t], o_recv.at[h, me], (view, t))

    for h in range(2):
        wait_far(1 + h)
        buf = (vlow, vhigh)[h]

        def sum_tiles(d, carry, h=h, buf=buf):
            ts = [lax.rem(me + 1 + 4 * d + n, toks) for n in range(4)]
            for t in ts:
                parts = []
                for j in range(NB):
                    parts += [buf[sets[j] - toks + paired(j, t, i)] for i in range(BAND)]
                weights = wbuf.at[t, pl.ds(h * TILE, TILE)]
                cut = (1 + BAND) * LANES
                both = jnp.concatenate([weights[:, LANES:cut], weights[:, cut:]], axis=0)
                acc = jnp.dot(both, jnp.concatenate(parts, axis=0), preferred_element_type=jnp.float32)
                first, second = acc[:TILE], acc[TILE:]
                obuf[h, t] = (
                    own_sum[h, t]
                    + jnp.where(low[:HD], first[:HD] + roll_half(second[:HD]), roll_half(first[HD:]) + second[HD:])
                ).astype(jnp.bfloat16)
            for t in ts:
                @pl.when(t != me)
                def _(t=t):
                    o_copy(h, t).start()

            return carry

        lax.fori_loop(0, 4, sum_tiles, 0)
        orecv[h, unit_of(me)] = obuf[h, me]

    for h in range(2):
        for d in range(1, 16):
            src = lax.rem(me + toks - d, toks)
            remote(obuf.at[0, 0], orecv.at[h, unit_of(src)], o_send.at[h, 0], o_recv.at[h, src], (view, src)).wait_recv()
    for s in range(2):
        role = first_slot if s == 0 else 1 - first_slot
        for p in range(8):
            upper_rows, lower_rows = swap_halves(orecv[0, p * 2 + role], orecv[1, p * 2 + role])
            out_ref[0, s, :HD, p * LANES:(p + 1) * LANES] = upper_rows
            out_ref[0, s, HD:, p * LANES:(p + 1) * LANES] = lower_rows

    for d in range(1, 16):
        peer = lax.rem(me + d, toks)
        for a in range(3):
            a2a_copy(a, peer).wait_send()
        for h in range(2):
            o_copy(h, peer).wait_send()
    for n in range(4):
        for hop, origin in ((0, 0), (1, 0), (2, -1), (3, 1)):
            z_tile(hop, n, origin).wait_send()
    for a in range(3):
        for hop in range(4):
            for gi in range(1 if a == 0 else 0, 4):
                z_copy(a, hop, gi, GX[gi]).wait_send()


def local(queries, keys, values, tile_mask, offsets, branch_slots):
    bf16 = jnp.bfloat16
    hbm = pl.BlockSpec(memory_space=pl.ANY)
    dma = pltpu.SemaphoreType.DMA
    return pl.pallas_call(
        attend_kernel,
        out_shape=jax.ShapeDtypeStruct(queries.shape, bf16),
        in_specs=[hbm] * 6,
        out_specs=pl.BlockSpec(memory_space=pltpu.VMEM),
        scratch_shapes=[
            pltpu.SMEM((1, NB, 16, 16), jnp.int32),
            pltpu.SMEM((1, NB), jnp.int32),
            pltpu.SMEM((2, 32), jnp.int32),
            pltpu.VMEM((2, TILE, 1024), bf16),
            pltpu.VMEM((2, TILE, 1024), bf16),
            pltpu.VMEM((2, TILE, 1024), bf16),
            pltpu.VMEM((16, TILE, LANES), bf16),
            pltpu.VMEM((16, 2, HD, LANES), bf16),
            pltpu.VMEM((16, TILE, LANES), bf16),
            pltpu.VMEM((16, TILE, LANES), bf16),
            pltpu.VMEM((80, TILE, LANES), bf16),
            pltpu.VMEM((16, 2, HD, LANES), bf16),
            pltpu.VMEM((64, HD, LANES), bf16),
            pltpu.VMEM((64, HD, LANES), bf16),
            pltpu.VMEM((2, 16, HD, LANES), jnp.float32),
            pltpu.VMEM((2 * TILE, KEY_COLS * LANES), jnp.float32),
            pltpu.VMEM((16, 2 * TILE, KEY_COLS * LANES), bf16),
            pltpu.VMEM((2, 16, HD, LANES), bf16),
            pltpu.VMEM((2, 16, HD, LANES), bf16),
            pltpu.SMEM((NB, 16), jnp.int32),
            pltpu.SMEM((NB, 16), jnp.int32),
            dma((6,)),
            dma((3, 16)),
            dma((3, 16)),
            dma((3, 4, 7)),
            dma((3, 4, 7)),
            dma((2, 16)),
            dma((2, 16)),
        ],
        compiler_params=pltpu.CompilerParams(
            collective_id=0, has_side_effects=True, vmem_limit_bytes=VMEM_BYTES
        ),
        cost_estimate=pl.CostEstimate(flops=3_500_000_000, bytes_accessed=2 << 20, transcendentals=7_000_000),
    )(tile_mask, offsets, branch_slots.T, queries, keys, values)


def solution(mesh):
    in_specs = (
        P("view", None, "tok", None),
        P("view", None, "tok", None),
        P("view", None, "tok", None),
        P("view", None, None, None),
        P("view", None),
        P(),
    )
    out_specs = P("view", None, "tok", None)
    return jax.shard_map(local, mesh=mesh, in_specs=in_specs, out_specs=out_specs, check_vma=False)
```

```python
import jax
import jax.numpy as jnp
from jax import lax
from jax.experimental import pallas as pl
from jax.experimental.pallas import tpu as pltpu
from jax.sharding import PartitionSpec as P

MESH = pl.DeviceIdType.MESH
TILE = 128
LANES = 128
HD = 64
BAND = 6
NB = 2
KEY_COLS = 1 + NB * BAND
NEG_SCORE = -1e30
VMEM_BYTES = 63 * 1024 * 1024
XS = 4
ROWS = 64
LOW_STEP = 1
HIGH_STEP = 11
GX = (0, 1, 3, 2)


def attend_kernel(
    mask_in, off_in, slot_in, q_ref, k_ref, v_ref, out_ref,
    mask_ref, off_ref, slot_ref,
    raw_k, raw_v, raw_q, stage_k, stage_v, stage_q, qbuf, kbuf, vown, vlow, vhigh, own_sum, sbuf, wbuf,
    obuf, orecv, start_s, count_s,
    in_sem, a_send, a_recv, z_send, z_recv, o_send, o_recv,
):
    views = lax.axis_size("view")
    toks = lax.axis_size("tok")
    group = toks // XS
    view = lax.axis_index("view")
    me = lax.axis_index("tok")
    right = lax.rem(view + 1, views)
    left = lax.rem(view + views - 1, views)
    my_x = me // group
    my_r = lax.rem(me, group)
    half = views // 2
    upper = view // half

    def flip(tok, by):
        return tok + by * (2 - 4 * lax.rem(tok // 2, 2))

    def unit_of(tok):
        return flip(tok, upper)

    right_dev = (right, flip(me, lax.rem(upper + right // half, 2)))
    left_dev = (left, flip(me, lax.rem(upper + left // half, 2)))
    raws = (raw_k, raw_v, raw_q)
    stages = (stage_k, stage_v, stage_q)
    bufs = (kbuf, vown, qbuf)

    def remote(src, dst, send, recv, dev):
        return pltpu.make_async_remote_copy(
            src_ref=src, dst_ref=dst, send_sem=send, recv_sem=recv, device_id=dev, device_id_type=MESH
        )

    def in_copy(a):
        return pltpu.make_async_copy((k_ref, v_ref, q_ref)[a].at[0], raws[a], in_sem.at[a])

    tables = [
        pltpu.make_async_copy(src, dst, in_sem.at[3 + n])
        for n, (src, dst) in enumerate(((slot_in, slot_ref), (off_in, off_ref), (mask_in, mask_ref)))
    ]
    tables[0].start()
    for a in range(3):
        in_copy(a).start()
    for table in tables[1:]:
        table.start()

    barrier = pltpu.get_barrier_semaphore()
    for to in (right_dev, left_dev):
        pl.semaphore_signal(barrier, inc=1, device_id=to, device_id_type=MESH)
    for d in range(1, 16):
        pl.semaphore_signal(barrier, inc=1, device_id=(view, lax.rem(me + d, toks)), device_id_type=MESH)

    tables[0].wait()
    first_slot = slot_ref[0, view]

    def swap_halves(x, y):
        return (
            jnp.concatenate([x[:, :HD], y[:, :HD]], axis=1),
            jnp.concatenate([x[:, HD:], y[:, HD:]], axis=1),
        )

    def stage_array(a):
        in_copy(a).wait()
        for b in range(2):
            slot = first_slot if b == 0 else 1 - first_slot
            for p in range(8):
                tile = raws[a][slot, :, p * LANES:(p + 1) * LANES]
                if a == 1:
                    low_head, high_head = swap_halves(tile[:HD], tile[HD:])
                    stage_v[p * 2 + b, 0] = low_head
                    stage_v[p * 2 + b, 1] = high_head
                else:
                    stages[a][p * 2 + b] = tile
        bufs[a][me] = stages[a][unit_of(me)]

    def mate(r, n):
        other = r + 1 - 2 * lax.rem(r, 2) if n % 2 else r
        return lax.rem(other + 2, group) if n >= 2 else other

    next_dev = (view, lax.rem(me + 1, toks))

    def a2a_send(a, columns=GX):
        for gx in columns:
            for n in range(4):
                if (gx, n) != (0, 0):
                    dest = lax.rem(my_x + gx, XS) * group + mate(my_r, n)
                    sem = 5 + a if a else n - 1 if gx == 0 else 2 + GX.index(gx)
                    remote(
                        stages[a].at[unit_of(dest)], bufs[a].at[me], a_send.at[a], a_recv.at[sem], (view, dest)
                    ).start()

    def a2a_all(a):
        part = pl.ds(0, 15)
        return remote(stages[a].at[part], bufs[a].at[part], a_send.at[a], a_recv.at[5 + a], next_dev)

    def a2a_wait_tile(n):
        src = my_x * group + mate(my_r, n)
        remote(stage_k.at[0], kbuf.at[src], a_send.at[0], a_recv.at[n - 1], next_dev).wait_recv()

    def a2a_wait_column(gi):
        part = pl.ds(lax.rem(my_x + XS - GX[gi], XS) * group, 4)
        remote(stage_k.at[pl.ds(0, 4)], kbuf.at[part], a_send.at[0], a_recv.at[2 + gi], next_dev).wait_recv()

    def z_recv_sem(a, hop, part):
        if hop >= 2:
            return z_recv.at[30 + a * 2 + hop - 2]
        return z_recv.at[(14 + (a - 1) * 8 + hop * 4 if a else hop * 7) + part]

    def z_copy(a, hop, gi, gx):
        start = lax.rem(my_x + XS - gx, XS) * group
        src_set, dst_set, dev = ((0, 1, right_dev), (0, 2, left_dev), (1, 3, right_dev), (2, 4, left_dev))[hop]
        if a == 0:
            src = kbuf.at[pl.ds(src_set * toks + start, 4)]
            dst = kbuf.at[pl.ds(dst_set * toks + start, 4)]
        else:
            buf = (vlow, vhigh)[a - 1]
            if hop < 2:
                src = vown.at[pl.ds(start, 4), a - 1]
            else:
                src = buf.at[pl.ds((src_set - 1) * toks + start, 4)]
            dst = buf.at[pl.ds((dst_set - 1) * toks + start, 4)]
        sem = gi + 3 if a == 0 else gi
        return remote(src, dst, z_send.at[a, hop], z_recv_sem(a, hop, sem), dev)

    def z_all(a, hop):
        dst_set, dev = ((1, right_dev), (2, left_dev), (3, right_dev), (4, left_dev))[hop]
        buf, lead = ((kbuf, 0), (vlow, 1), (vhigh, 1))[a]
        part = buf.at[pl.ds((dst_set - lead) * toks, 16)]
        return remote(part, part, z_send.at[a, hop], z_recv_sem(a, hop, 0), dev)

    def unit_place(by):
        return lax.rem(flip(me, lax.rem(upper + lax.rem(view + views + by, views) // half, 2)), group)

    def z_tile(hop, n, origin):
        tile = my_x * group + mate(unit_place(origin), n)
        src_set, dst_set, dev = ((0, 1, right_dev), (0, 2, left_dev), (1, 3, right_dev), (2, 4, left_dev))[hop]
        return remote(
            kbuf.at[src_set * toks + tile], kbuf.at[dst_set * toks + tile],
            z_send.at[0, hop], z_recv_sem(0, hop, n), dev,
        )

    def send_tile(n):
        for hop in (0, 1):
            z_tile(hop, n, 0).start()

    def send_tile_on(n):
        for hop, origin in ((0, -1), (1, 1)):
            z_tile(hop, n, origin).wait_recv()
            z_tile(hop + 2, n, origin).start()

    def send_own(a, gi, gx):
        for hop in (0, 1):
            z_copy(a, hop, gi, gx).start()

    def send_on(a, gi, gx):
        for hop in (0, 1):
            z_copy(a, hop, gi, gx).wait_recv()
            z_copy(a, hop + 2, gi, gx).start()

    def wait_far(a):
        for hop in (2, 3):
            z_all(a, hop).wait_recv()

    stage_array(0)
    pl.semaphore_wait(barrier, 17)
    send_tile(0)
    a2a_send(0, (0,))
    a2a_send(0, (1, 3))
    for n in range(1, 4):
        a2a_wait_tile(n)
        send_tile(n)
    a2a_send(0, (2,))
    stage_array(1)
    for gi in (1, 2):
        a2a_wait_column(gi)
        send_own(0, gi, GX[gi])
    stage_array(2)
    a2a_send(1)
    a2a_send(2)
    a2a_wait_column(3)
    send_own(0, 3, GX[3])
    for n in range(4):
        send_tile_on(n)
    for gi in range(1, 4):
        send_on(0, gi, GX[gi])
    a2a_all(1).wait_recv()
    for gi in range(4):
        send_own(1, gi, GX[gi])

    for table in tables[1:]:
        table.wait()

    for j in range(NB):
        def count_row(t, carry, j=j):
            first = jnp.int32(0)
            total = jnp.int32(0)
            before = mask_ref[0, j, t, 15]
            for k in range(16):
                here = mask_ref[0, j, t, k]
                total = total + here
                first = first + jnp.where((here == 1) & (before == 0), k, 0)
                before = here
            start_s[j, t] = first
            count_s[j, t] = total
            return carry
        lax.fori_loop(0, 16, count_row, 0)

    a2a_all(2).wait_recv()
    wait_far(0)

    sets = []
    for j in range(NB):
        off = off_ref[0, j]
        sets.append(jnp.where(off == -1, 1, jnp.where(off == 1, 2, jnp.where(off == -2, 3, 4))) * toks)
    low = lax.broadcasted_iota(jnp.int32, (TILE, LANES), 1) < HD
    low_row = lax.broadcasted_iota(jnp.int32, (1, LANES), 1) < HD

    def roll_half(x):
        return jnp.concatenate([x[:, HD:], x[:, :HD]], axis=1)

    def paired(j, t, i):
        return lax.rem(start_s[j, t] + i, 16)

    def dot_t(x, y):
        return lax.dot_general(x, y, (((1,), (1,)), ((), ())), preferred_element_type=jnp.float32)

    def weigh_tile(t):
        q = qbuf[t] * jnp.bfloat16(0.125)
        zero = jnp.zeros_like(q)
        both = jnp.concatenate([jnp.where(low, q, zero), jnp.where(low, zero, q)], axis=0)
        sbuf[:, :LANES] = dot_t(both, kbuf[t])
        for j in range(NB):
            for i in range(0, BAND, 2):
                one, two = kbuf[sets[j] + paired(j, t, i)], kbuf[sets[j] + paired(j, t, i + 1)]
                s = dot_t(both, jnp.concatenate([one[:HD], two[:HD], one[HD:], two[HD:]], axis=0))
                bias = jnp.where(
                    low_row,
                    jnp.where(i < count_s[j, t], jnp.float32(0), jnp.float32(NEG_SCORE)),
                    jnp.where(i + 1 < count_s[j, t], jnp.float32(0), jnp.float32(NEG_SCORE)),
                )
                for h in range(2):
                    c = 1 + h * BAND + (j * BAND + i) // 2
                    sbuf[:, c * LANES:(c + 1) * LANES] = s[:, h * LANES:(h + 1) * LANES] + bias
        for rb in range(0, 2 * TILE, ROWS):
            rows = pl.ds(rb, ROWS)
            top = sbuf[rows, :LANES]
            for c in range(1, KEY_COLS):
                top = jnp.maximum(top, sbuf[rows, c * LANES:(c + 1) * LANES])
            top = jnp.max(top, axis=1, keepdims=True)
            total = jnp.zeros((ROWS, LANES), jnp.float32)
            for c in range(KEY_COLS):
                e = jnp.exp(sbuf[rows, c * LANES:(c + 1) * LANES] - top)
                sbuf[rows, c * LANES:(c + 1) * LANES] = e
                total = total + e
            inv = 1.0 / jnp.sum(total, axis=1, keepdims=True)
            for c in range(KEY_COLS):
                wbuf[t, rows, c * LANES:(c + 1) * LANES] = (
                    sbuf[rows, c * LANES:(c + 1) * LANES] * inv
                ).astype(jnp.bfloat16)
        for h in range(2):
            pack = vown[t, h]
            part = jnp.dot(
                wbuf[t, h * TILE:(h + 1) * TILE, :LANES], jnp.concatenate([pack, roll_half(pack)], axis=0),
                preferred_element_type=jnp.float32,
            )
            own_sum[h, t] = jnp.concatenate([part[:HD, :HD], part[HD:, :HD]], axis=1)

    def gx_of(gi):
        return gi + (gi // 2) * (1 - 2 * lax.rem(gi, 2))

    def weigh_step(t, carry):
        weigh_tile(t)

        @pl.when((t >= LOW_STEP) & (t < LOW_STEP + 4))
        def _():
            gi = t - LOW_STEP
            send_on(1, gi, gx_of(gi))
            send_own(2, gi, gx_of(gi))

        @pl.when((t >= HIGH_STEP) & (t < HIGH_STEP + 4))
        def _():
            gi = t - HIGH_STEP
            send_on(2, gi, gx_of(gi))

        return carry

    lax.fori_loop(0, 16, weigh_step, 0)

    def o_copy(h, t):
        return remote(obuf.at[h, t], orecv.at[h, unit_of(me)], o_send.at[h], o_recv.at[h], (view, t))

    def o_all(h):
        part = pl.ds(0, 15)
        return remote(obuf.at[h, part], orecv.at[h, part], o_send.at[h], o_recv.at[h], next_dev)

    for h in range(2):
        wait_far(1 + h)
        buf = (vlow, vhigh)[h]

        def sum_tiles(d, carry, h=h, buf=buf):
            ts = [lax.rem(me + 1 + 4 * d + n, toks) for n in range(4)]
            for t in ts:
                parts = []
                for j in range(NB):
                    parts += [buf[sets[j] - toks + paired(j, t, i)] for i in range(BAND)]
                weights = wbuf.at[t, pl.ds(h * TILE, TILE)]
                cut = (1 + BAND) * LANES
                both = jnp.concatenate([weights[:, LANES:cut], weights[:, cut:]], axis=0)
                acc = jnp.dot(both, jnp.concatenate(parts, axis=0), preferred_element_type=jnp.float32)
                first, second = acc[:TILE], acc[TILE:]
                obuf[h, t] = (
                    own_sum[h, t]
                    + jnp.where(low[:HD], first[:HD] + roll_half(second[:HD]), roll_half(first[HD:]) + second[HD:])
                ).astype(jnp.bfloat16)
            for t in ts:
                @pl.when(t != me)
                def _(t=t):
                    o_copy(h, t).start()

            return carry

        lax.fori_loop(0, 4, sum_tiles, 0)
        orecv[h, unit_of(me)] = obuf[h, me]

    for h in range(2):
        o_all(h).wait_recv()
    for s in range(2):
        role = first_slot if s == 0 else 1 - first_slot
        for p in range(8):
            upper_rows, lower_rows = swap_halves(orecv[0, p * 2 + role], orecv[1, p * 2 + role])
            out_ref[0, s, :HD, p * LANES:(p + 1) * LANES] = upper_rows
            out_ref[0, s, HD:, p * LANES:(p + 1) * LANES] = lower_rows

    for a in range(3):
        a2a_all(a).wait_send()
        for hop in range(4):
            z_all(a, hop).wait_send()
    for h in range(2):
        o_all(h).wait_send()


def local(queries, keys, values, tile_mask, offsets, branch_slots):
    bf16 = jnp.bfloat16
    hbm = pl.BlockSpec(memory_space=pl.ANY)
    dma = pltpu.SemaphoreType.DMA
    return pl.pallas_call(
        attend_kernel,
        out_shape=jax.ShapeDtypeStruct(queries.shape, bf16),
        in_specs=[hbm] * 6,
        out_specs=pl.BlockSpec(memory_space=pltpu.VMEM),
        scratch_shapes=[
            pltpu.SMEM((1, NB, 16, 16), jnp.int32),
            pltpu.SMEM((1, NB), jnp.int32),
            pltpu.SMEM((2, 32), jnp.int32),
            pltpu.VMEM((2, TILE, 1024), bf16),
            pltpu.VMEM((2, TILE, 1024), bf16),
            pltpu.VMEM((2, TILE, 1024), bf16),
            pltpu.VMEM((16, TILE, LANES), bf16),
            pltpu.VMEM((16, 2, HD, LANES), bf16),
            pltpu.VMEM((16, TILE, LANES), bf16),
            pltpu.VMEM((16, TILE, LANES), bf16),
            pltpu.VMEM((80, TILE, LANES), bf16),
            pltpu.VMEM((16, 2, HD, LANES), bf16),
            pltpu.VMEM((64, HD, LANES), bf16),
            pltpu.VMEM((64, HD, LANES), bf16),
            pltpu.VMEM((2, 16, HD, LANES), jnp.float32),
            pltpu.VMEM((2 * TILE, KEY_COLS * LANES), jnp.float32),
            pltpu.VMEM((16, 2 * TILE, KEY_COLS * LANES), bf16),
            pltpu.VMEM((2, 16, HD, LANES), bf16),
            pltpu.VMEM((2, 16, HD, LANES), bf16),
            pltpu.SMEM((NB, 16), jnp.int32),
            pltpu.SMEM((NB, 16), jnp.int32),
            dma((6,)),
            dma((3,)),
            dma((8,)),
            dma((3, 4)),
            dma((36,)),
            dma((2,)),
            dma((2,)),
        ],
        compiler_params=pltpu.CompilerParams(
            collective_id=0, has_side_effects=True, vmem_limit_bytes=VMEM_BYTES
        ),
        cost_estimate=pl.CostEstimate(flops=3_500_000_000, bytes_accessed=2 << 20, transcendentals=7_000_000),
    )(tile_mask, offsets, branch_slots.T, queries, keys, values)


def solution(mesh):
    in_specs = (
        P("view", None, "tok", None),
        P("view", None, "tok", None),
        P("view", None, "tok", None),
        P("view", None, None, None),
        P("view", None),
        P(),
    )
    out_specs = P("view", None, "tok", None)
    return jax.shard_map(local, mesh=mesh, in_specs=in_specs, out_specs=out_specs, check_vma=False)
```
